512 devices in a mesh: seq: 64 (over x, y, z_hi, core), tp: 8 (over z_lo).
Axes of the slice: x: 4, y: 4, z: 16 (z_hi: 2, z_lo: 8; z = z_hi * 8 + z_lo), core: 2. Of those that a mesh axis runs over, the one named last changes fastest.
Arguments:
- queries: bfloat16 [16384, 3072], P(('seq', 'tp')), may hold values from -6 to 6
- keys: bfloat16 [16384, 3072], P(('seq', 'tp')), may hold values from -6 to 6
- values: bfloat16 [16384, 3072], P(('seq', 'tp')), may hold values from -6 to 6
- out_grad: bfloat16 [16384, 3072], P(('seq', 'tp')), may hold values from -6 to 6
- tile_image: int32 [128], replicated, may hold values from 0 to 63, never falling along the last dimension, each value on 1 to 3 neighbouring positions
- pad_count: int32 [64], replicated, may hold values from 0 to 126
Outputs:
- attended: bfloat16 [16384, 3072], P('seq', 'tp')
- query_grad: bfloat16 [16384, 3072], P('seq', 'tp')
- key_grad: bfloat16 [16384, 3072], P('seq', 'tp')
- value_grad: bfloat16 [16384, 3072], P('seq', 'tp')
The draws below stay inside these ranges and needn't reach their ends.
Inputs may be any that keep to these rules, and one draw needn't show every extreme that they name: `tile_image`: never falls along the pack; every image number owns 1 to 3 consecutive tiles, and some image owns exactly 3.
All inputs are finite; a program needn't handle non-finite values.
Results may differ from the reference program's by a relative error of at most 0.03.
Values may be sent and summed in bfloat16 or wider, within the bound.
No kernel may reach another device: no remote copies, remote signals or barrier semaphores. Data moves between devices by JAX's collectives and lax.ppermute only.
A program may use at most 64 MiB of HBM per device.

```python
import math
import jax
import jax.numpy as jnp
import numpy as np
from jax import lax

HEADS = 24
HEAD_DIM = 128
SEQ_ROWS = 256
TILE = 128
REACH = 1
TILES = 128
IMAGE_TILES = 3
IMAGES = 64
TOKENS = 16384
N_SEQ = 64


def draw_queries(key, part):
    key = jax.random.fold_in(key, 3)
    shape4 = (TILES, TILE, HEADS, HEAD_DIM)
    base_draw = jnp.clip(jax.random.normal(key, shape4), -6.0, 6.0)
    return base_draw.reshape(TOKENS, HEADS * HEAD_DIM).astype(jnp.bfloat16)


def draw_keys(key, part):
    key = jax.random.fold_in(key, 5)
    shape4 = (TILES, TILE, HEADS, HEAD_DIM)
    base_draw = jnp.clip(jax.random.normal(key, shape4), -6.0, 6.0)
    return base_draw.reshape(TOKENS, HEADS * HEAD_DIM).astype(jnp.bfloat16)


def plant(drawn, own_key, least, high):
    dims = drawn.shape
    spot = [jax.random.randint(jax.random.fold_in(own_key, axis), (), 0, dims[axis]) for axis in range(len(dims))]
    drawn = drawn.at[tuple(spot)].set(least)
    longest = dims.index(max(dims))
    spot[longest] = (spot[longest] + 1) % dims[longest]
    return drawn.at[tuple(spot)].set(high)


def level_of(key, dims, cuts, low, largest):
    factor_of, own = 1.0, jax.random.fold_in(key, 6)
    for axis_at, shards_of in cuts:
        draws = jnp.exp(jax.random.uniform(jax.random.fold_in(own, axis_at), (shards_of,), jnp.float32, low / len(cuts), largest / len(cuts)))
        factor_of = factor_of * jnp.repeat(draws, dims[axis_at] // shards_of).reshape([-1 if axis == axis_at else 1 for axis in range(len(dims))])
    return factor_of


def profile(amount, total, most, slope):
    portions = [(1 << 20) // math.isqrt(standing ** slope) + 1 for standing in range(2, amount + 1)]
    surplus, holding = total - most - (amount - 1), [1] * (amount - 1)
    while surplus > 0:
        movable = [i for i in range(amount - 1) if holding[i] < most]
        pool, remaining = sum([portions[i] for i in movable]), surplus
        for i in movable:
            more = min(most - holding[i], max(1, remaining * portions[i] // pool), surplus)
            holding[i] = holding[i] + more
            surplus = surplus - more
    return np.array([most] + holding)


def uneven(key, count, total, bound, lean):
    if count == 2:
        one = jax.random.randint(key, (), max(1, total - bound), min(bound, total - 1) + 1)
        return jnp.stack([one, total - one])
    sizes = jnp.asarray(profile(count, total, bound, lean), jnp.int32)
    pairs = (count - 1) // 2
    giver, sink = sizes[1:1 + 2 * pairs:2], sizes[2:2 + 2 * pairs:2]
    room = jnp.minimum(giver - 1, bound - sink)
    shifted = jax.random.randint(jax.random.fold_in(key, 1), (pairs,), 0, 1 << 20) % (room + 1)
    sizes = sizes.at[1:1 + 2 * pairs:2].set(giver - shifted).at[2:2 + 2 * pairs:2].set(sink + shifted)
    return sizes[jax.random.permutation(jax.random.fold_in(key, 2), count)]


def gaussian(key, extent, width, bound, cuts=(), kind=jnp.bfloat16):
    values = width * jax.random.normal(key, extent, jnp.float32)
    if cuts:
        values = values * level_of(key, extent, cuts, -0.22, 0.18)
    return jnp.clip(values, -bound, bound).astype(kind)


def setup_inputs(seed: int = 0) -> dict:
    key_of = jax.random.split(jax.random.key(seed), 7)
    queries = draw_queries(jax.random.fold_in(key_of[6], 71), 0)
    keys = draw_keys(jax.random.fold_in(key_of[6], 71), 0)
    values = gaussian(key_of[2], (TOKENS, HEADS * HEAD_DIM), 1.0, 6.0, ((0, 512),))
    out_grad = gaussian(key_of[3], (TOKENS, HEADS * HEAD_DIM), 1.0, 6.0, ((0, 512),))
    tile_image = jnp.searchsorted(jnp.cumsum(uneven(key_of[4], IMAGES, TILES, IMAGE_TILES, 2)), jnp.arange(TILES), side="right").astype(jnp.int32)
    pad_count = plant(jax.random.randint(key_of[5], (IMAGES,), 0, TILE - 1), jax.random.fold_in(key_of[5], 1), 0, (TILE - 1) - 1).astype(jnp.int32)
    return dict(queries=queries, keys=keys, values=values, out_grad=out_grad, tile_image=tile_image, pad_count=pad_count)


masked_score = -1.0e30


def rounded(array):
    return lax.optimization_barrier(array.astype(jnp.bfloat16)).astype(jnp.float32)


def token_layout(tile_image, pad_count):
    image_index = jnp.arange(IMAGES, dtype=jnp.int32)
    stop_tiles = jnp.sum((tile_image[None, :] <= image_index[:, None]).astype(jnp.int32), axis=1).astype(jnp.int32)
    end_tokens = (stop_tiles * TILE - pad_count).astype(jnp.int32)
    tile_limit = jnp.sum(jnp.where(tile_image[:, None] == image_index[None, :], end_tokens[None, :], 0), axis=1).astype(jnp.int32)
    token_image = jnp.repeat(tile_image, TILE)
    token_valid = jnp.arange(TOKENS, dtype=jnp.int32) < jnp.repeat(tile_limit, TILE)
    return token_image, token_valid


def pair_mask(query_image, query_valid, key_image, key_valid):
    return (query_image[:, None] == key_image[None, :]) & query_valid[:, None] & key_valid[None, :]


def pair_scores(query_block, key_block, allowed, scaling):
    raw_scores = jnp.einsum("qhd,khd->hqk", query_block.astype(jnp.float32), key_block.astype(jnp.float32))
    return jnp.where(allowed[None], raw_scores * scaling, masked_score)


def reference(queries, keys, values, out_grad, tile_image, pad_count):
    scaling = HEAD_DIM ** -0.5
    token_image, token_valid = token_layout(tile_image, pad_count)
    margin = REACH * SEQ_ROWS
    window = (2 * REACH + 1) * SEQ_ROWS
    shape3 = (TOKENS, HEADS, HEAD_DIM)
    query3 = queries.reshape(shape3)
    key3 = keys.reshape(shape3)
    value3 = values.reshape(shape3)
    grad3 = out_grad.reshape(shape3)

    def widen_rows(array):
        return jnp.pad(array, ((margin, margin), (0, 0), (0, 0)))

    wide_queries = widen_rows(query3)
    wide_keys = widen_rows(key3)
    wide_values = widen_rows(value3)
    wide_grad = widen_rows(grad3)
    wide_image = jnp.pad(token_image, margin, constant_values=-1)
    wide_valid = jnp.pad(token_valid, margin)
    first_rows = jnp.arange(N_SEQ, dtype=jnp.int32) * SEQ_ROWS

    def own_rows(array, first_row):
        return lax.dynamic_slice_in_dim(array, first_row, SEQ_ROWS, 0)

    def wide_rows(array, first_row):
        return lax.dynamic_slice_in_dim(array, first_row, window, 0)

    def shard_mask(first_row):
        return pair_mask(own_rows(token_image, first_row), own_rows(token_valid, first_row),
                         wide_rows(wide_image, first_row), wide_rows(wide_valid, first_row))

    def forward_shard(first_row):
        allowed = shard_mask(first_row)
        scores = pair_scores(own_rows(query3, first_row), wide_rows(wide_keys, first_row), allowed, scaling)
        row_top = jnp.max(scores, axis=2, keepdims=True)
        log_total = row_top[:, :, 0] + jnp.log(jnp.sum(jnp.exp(scores - row_top), axis=2))
        weights = jnp.where(allowed[None], jnp.exp(scores - log_total[:, :, None]), 0.0)
        attended = jnp.einsum("hqk,khd->qhd", rounded(weights), wide_rows(wide_values, first_row).astype(jnp.float32))
        grad_dot = jnp.einsum("qhd,qhd->hq", own_rows(grad3, first_row).astype(jnp.float32), rounded(attended))
        return attended.astype(jnp.bfloat16), log_total, grad_dot

    attended, log_total, grad_dot = lax.map(forward_shard, first_rows)
    attended = attended.reshape(TOKENS, HEADS * HEAD_DIM)
    log_total = jnp.transpose(log_total, (1, 0, 2)).reshape(HEADS, TOKENS)
    grad_dot = jnp.transpose(grad_dot, (1, 0, 2)).reshape(HEADS, TOKENS)

    def query_shard(first_row):
        allowed = shard_mask(first_row)
        window_keys = wide_rows(wide_keys, first_row)
        scores = pair_scores(own_rows(query3, first_row), window_keys, allowed, scaling)
        own_total = lax.dynamic_slice_in_dim(log_total, first_row, SEQ_ROWS, 1)
        own_dot = lax.dynamic_slice_in_dim(grad_dot, first_row, SEQ_ROWS, 1)
        weights = jnp.where(allowed[None], jnp.exp(scores - own_total[:, :, None]), 0.0)
        value_score = jnp.einsum("qhd,khd->hqk", own_rows(grad3, first_row).astype(jnp.float32),
                                 wide_rows(wide_values, first_row).astype(jnp.float32))
        score_grad = weights * (value_score - own_dot[:, :, None])
        result = jnp.einsum("hqk,khd->qhd", rounded(score_grad), window_keys.astype(jnp.float32)) * scaling
        return result.astype(jnp.bfloat16)

    query_grad = lax.map(query_shard, first_rows).reshape(TOKENS, HEADS * HEAD_DIM)
    wide_total = jnp.pad(log_total, ((0, 0), (margin, margin)))
    wide_dot = jnp.pad(grad_dot, ((0, 0), (margin, margin)))

    def key_shard(first_row):
        allowed = pair_mask(wide_rows(wide_image, first_row), wide_rows(wide_valid, first_row),
                            own_rows(token_image, first_row), own_rows(token_valid, first_row))
        window_queries = wide_rows(wide_queries, first_row)
        window_grad = wide_rows(wide_grad, first_row)
        scores = pair_scores(window_queries, own_rows(key3, first_row), allowed, scaling)
        window_total = lax.dynamic_slice_in_dim(wide_total, first_row, window, 1)
        window_dot = lax.dynamic_slice_in_dim(wide_dot, first_row, window, 1)
        weights = jnp.where(allowed[None], jnp.exp(scores - window_total[:, :, None]), 0.0)
        value_score = jnp.einsum("qhd,khd->hqk", window_grad.astype(jnp.float32),
                                 own_rows(value3, first_row).astype(jnp.float32))
        score_grad = weights * (value_score - window_dot[:, :, None])
        key_part = jnp.einsum("hqk,qhd->khd", rounded(score_grad), window_queries.astype(jnp.float32)) * scaling
        value_part = jnp.einsum("hqk,qhd->khd", rounded(weights), window_grad.astype(jnp.float32))
        return key_part.astype(jnp.bfloat16), value_part.astype(jnp.bfloat16)

    key_grad, value_grad = lax.map(key_shard, first_rows)
    key_grad = key_grad.reshape(TOKENS, HEADS * HEAD_DIM)
    value_grad = value_grad.reshape(TOKENS, HEADS * HEAD_DIM)
    return attended, query_grad, key_grad, value_grad
```

```python
import jax
import jax.numpy as jnp
from jax import lax
from jax.experimental import pallas as pl
from jax.experimental.pallas import tpu as pltpu
from jax.sharding import PartitionSpec as P

HEAD_DIM = 128
TILE = 128
WINDOW = 3
BF16 = jnp.bfloat16
F32 = jnp.float32


def image_ends(tile_image, pad_count):
    image_index = jnp.arange(pad_count.shape[0], dtype=jnp.int32)
    stop_tiles = jnp.sum((tile_image[None, :] <= image_index[:, None]).astype(jnp.int32), axis=1)
    return stop_tiles * TILE - pad_count


def tile_plan(tile_image, pad_count, seq_index, tile_count):
    ends = image_ends(tile_image, pad_count)
    tiles = jnp.arange(tile_image.shape[0], dtype=jnp.int32)
    images = jnp.arange(pad_count.shape[0], dtype=jnp.int32)
    plan = []
    for tile in range(tile_count):
        place = seq_index * tile_count + tile
        image = jnp.sum(jnp.where(tiles == place, tile_image, 0))
        first = jnp.sum((tile_image < image).astype(jnp.int32))
        end = jnp.sum(jnp.where(images == image, ends, 0))
        back = place - first
        plan += [tile_count + tile - back, back, end - first * TILE]
    return jnp.stack(plan).astype(jnp.int32)


def attention_kernel(
    plan_ref, near_ref, pair_ref, attended_ref, query_ref, key_ref, value_ref, rows, weight_buf, grad_buf, sems
):
    heads = attended_ref.shape[1] // HEAD_DIM
    tile_count = attended_ref.shape[0] // TILE
    near_chunks, pair_chunks = near_ref.shape[0], pair_ref.shape[0]
    chunk = near_ref.shape[2]
    per_tile = TILE // chunk
    scaling = HEAD_DIM ** (-0.5)
    near_at, pair_at = plan_ref[3 * tile_count], plan_ref[3 * tile_count + 1]
    copies = (
        pltpu.make_async_copy(pair_ref, rows.at[pl.ds(pair_at, pair_chunks)], sems.at[0]),
        pltpu.make_async_copy(near_ref, rows.at[pl.ds(near_at, near_chunks)], sems.at[1]),
    )
    for copy in copies:
        copy.start()
    for copy in copies:
        copy.wait()
    contract_last = (((1,), (1,)), ((), ()))
    contract_first = (((0,), (0,)), ((), ()))

    def dot(left, right, dims):
        return lax.dot_general(left, right, dims, preferred_element_type=F32)

    column = lax.broadcasted_iota(jnp.int32, (TILE, WINDOW * TILE), 1)
    row = lax.broadcasted_iota(jnp.int32, (TILE, 1), 0)
    for tile in range(tile_count):
        start, back, live = plan_ref[3 * tile], plan_ref[3 * tile + 1], plan_ref[3 * tile + 2]
        seen = column < live
        own = pl.ds(tile * TILE, TILE)
        own_window = pl.ds(pl.multiple_of(back * TILE, TILE), TILE)
        for head in range(heads):
            lanes = slice(head * HEAD_DIM, (head + 1) * HEAD_DIM)

            def part(index, first, count):
                block = rows[pl.ds(first * per_tile, count * per_tile), index, :, lanes]
                return block.reshape(count * TILE, HEAD_DIM)

            keys, values = part(1, start, WINDOW), part(2, start, WINDOW)
            for step in range(WINDOW):
                queries, grads = part(0, start + step, 1), part(3, start + step, 1)
                scores = jnp.where(seen, dot(queries, keys, contract_last) * scaling, -1e30)
                top = jnp.max(scores, axis=1, keepdims=True)
                raised = jnp.exp(scores - top)
                total = jnp.sum(raised, axis=1, keepdims=True)
                inverse = jnp.where(row + step * TILE < live, 1.0 / total, 0.0)
                weights = raised * inverse
                value_score = dot(grads, values, contract_last)
                grad_dot = jnp.sum(weights * value_score, axis=1, keepdims=True)
                score_grad = weights * (value_score - grad_dot)
                weight_buf[step * TILE : (step + 1) * TILE, :] = weights.astype(BF16)
                grad_buf[step * TILE : (step + 1) * TILE, :] = score_grad.astype(BF16)
            queries, grads = part(0, start, WINDOW), part(3, start, WINDOW)
            attended_ref[own, lanes] = jnp.dot(weight_buf[own_window, :], values, preferred_element_type=F32).astype(BF16)
            query_ref[own, lanes] = (jnp.dot(grad_buf[own_window, :], keys, preferred_element_type=F32) * scaling).astype(BF16)
            key_ref[own, lanes] = (dot(grad_buf[:, own_window], queries, contract_first) * scaling).astype(BF16)
            value_ref[own, lanes] = dot(weight_buf[:, own_window], grads, contract_first).astype(BF16)


def body(queries, keys, values, out_grad, tile_image, pad_count):
    seq_index = lax.axis_index("seq")
    seq_size, tp_size = lax.axis_size("seq"), lax.axis_size("tp")
    chunk, width = queries.shape
    lanes = width // tp_size
    row_count = chunk * tp_size
    tile_count = row_count // TILE
    packed = jnp.stack([array.reshape(chunk, tp_size, lanes) for array in (queries, keys, values, out_grad)])
    packed = packed.transpose(2, 0, 1, 3)
    doubled = jnp.concatenate([packed, packed])
    groups = [
        [seq % seq_size * tp_size + tp for seq in (left, left + 1) for tp in range(tp_size)]
        for left in range(1, seq_size, 2)
    ]
    pair = lax.all_to_all(
        doubled, ("seq", "tp"), split_axis=0, concat_axis=0, tiled=True, axis_index_groups=groups
    )
    is_right = 1 - seq_index % 2
    own = lax.dynamic_slice_in_dim(pair, is_right * tp_size, tp_size, 0)
    swaps = [(left, left + 1) for left in range(0, seq_size, 2)]
    near = lax.ppermute(own, "seq", swaps + [(right, left) for left, right in swaps])
    plan = tile_plan(tile_image, pad_count, seq_index, tile_count)
    places = jnp.stack([is_right * 2 * tp_size, (1 - is_right) * tp_size]).astype(jnp.int32)
    plan = jnp.concatenate([plan, places])
    out = jax.ShapeDtypeStruct((row_count, lanes), BF16)
    vmem = pl.BlockSpec(memory_space=pltpu.VMEM)
    return pl.pallas_call(
        attention_kernel,
        out_shape=[out] * 4,
        in_specs=[
            pl.BlockSpec(memory_space=pltpu.SMEM),
            pl.BlockSpec(memory_space=pl.ANY),
            pl.BlockSpec(memory_space=pl.ANY),
        ],
        out_specs=[vmem] * 4,
        scratch_shapes=[
            pltpu.VMEM((3 * tp_size, 4, chunk, lanes), BF16),
            pltpu.VMEM((WINDOW * TILE, WINDOW * TILE), BF16),
            pltpu.VMEM((WINDOW * TILE, WINDOW * TILE), BF16),
            pltpu.SemaphoreType.DMA((2,)),
        ],
        compiler_params=pltpu.CompilerParams(vmem_limit_bytes=32 * 1024 * 1024),
    )(plan, near, pair)


def solution(mesh):
    rows = P(("seq", "tp"), None)
    out = P("seq", "tp")
    return jax.shard_map(
        body, mesh=mesh, in_specs=(rows,) * 4 + (P(), P()), out_specs=(out,) * 4, check_vma=False
    )
```

```python
import jax
import jax.numpy as jnp
from jax import lax
from jax.experimental import pallas as pl
from jax.experimental.pallas import tpu as pltpu
from jax.sharding import PartitionSpec as P

HEAD_DIM = 128
TILE = 128
WINDOW = 3
BF16 = jnp.bfloat16
F32 = jnp.float32


def pack_kernel(queries_ref, keys_ref, values_ref, grads_ref, packed_ref):
    count = packed_ref.shape[0] // 2
    lanes = packed_ref.shape[3]
    for index, source in enumerate((queries_ref, keys_ref, values_ref, grads_ref)):
        for place in range(count):
            block = source[:, place * lanes : (place + 1) * lanes]
            packed_ref[place, index] = block
            packed_ref[place + count, index] = block


def image_window(tile_image_ref, pad_count_ref, place):
    last = tile_image_ref.shape[0] - 1
    image = tile_image_ref[place]

    def same(step):
        inside = (place + step >= 0) & (place + step <= last)
        return (inside & (tile_image_ref[jnp.clip(place + step, 0, last)] == image)).astype(jnp.int32)

    back = same(-1) + same(-2)
    return back, (back + 1 + same(1) + same(2)) * TILE - pad_count_ref[image]


def attention_kernel(
    tile_image_ref, pad_count_ref, near_ref, pair_ref, attended_ref, query_ref, key_ref, value_ref, rows, weight_buf, grad_buf, sems
):
    heads = attended_ref.shape[1] // HEAD_DIM
    tile_count = attended_ref.shape[0] // TILE
    near_chunks, pair_chunks = near_ref.shape[0], pair_ref.shape[0]
    chunk = near_ref.shape[2]
    per_tile = TILE // chunk
    scaling = HEAD_DIM ** (-0.5)
    seq_index = lax.axis_index("seq")
    is_right = 1 - lax.rem(seq_index, 2)
    near_at, pair_at = is_right * pair_chunks, (1 - is_right) * near_chunks
    copies = (
        pltpu.make_async_copy(pair_ref, rows.at[pl.ds(pair_at, pair_chunks)], sems.at[0]),
        pltpu.make_async_copy(near_ref, rows.at[pl.ds(near_at, near_chunks)], sems.at[1]),
    )
    for copy in copies:
        copy.start()
    for copy in copies:
        copy.wait()
    contract_last = (((1,), (1,)), ((), ()))
    contract_first = (((0,), (0,)), ((), ()))

    def dot(left, right, dims):
        return lax.dot_general(left, right, dims, preferred_element_type=F32)

    column = lax.broadcasted_iota(jnp.int32, (TILE, WINDOW * TILE), 1)
    row = lax.broadcasted_iota(jnp.int32, (TILE, 1), 0)
    for tile in range(tile_count):
        back, live = image_window(tile_image_ref, pad_count_ref, seq_index * tile_count + tile)
        start = tile_count + tile - back
        seen = column < live
        own = pl.ds(tile * TILE, TILE)
        own_window = pl.ds(pl.multiple_of(back * TILE, TILE), TILE)
        for head in range(heads):
            lanes = slice(head * HEAD_DIM, (head + 1) * HEAD_DIM)

            def part(index, first, count):
                block = rows[pl.ds(first * per_tile, count * per_tile), index, :, lanes]
                return block.reshape(count * TILE, HEAD_DIM)

            keys, values = part(1, start, WINDOW), part(2, start, WINDOW)
            for step in range(WINDOW):
                queries, grads = part(0, start + step, 1), part(3, start + step, 1)
                scores = jnp.where(seen, dot(queries, keys, contract_last) * scaling, -1e30)
                top = jnp.max(scores, axis=1, keepdims=True)
                raised = jnp.exp(scores - top)
                total = jnp.sum(raised, axis=1, keepdims=True)
                inverse = jnp.where(row + step * TILE < live, 1.0 / total, 0.0)
                weights = raised * inverse
                value_score = dot(grads, values, contract_last)
                grad_dot = jnp.sum(weights * value_score, axis=1, keepdims=True)
                score_grad = weights * (value_score - grad_dot)
                weight_buf[step * TILE : (step + 1) * TILE, :] = weights.astype(BF16)
                grad_buf[step * TILE : (step + 1) * TILE, :] = score_grad.astype(BF16)
            queries, grads = part(0, start, WINDOW), part(3, start, WINDOW)
            attended_ref[own, lanes] = jnp.dot(weight_buf[own_window, :], values, preferred_element_type=F32).astype(BF16)
            query_ref[own, lanes] = (jnp.dot(grad_buf[own_window, :], keys, preferred_element_type=F32) * scaling).astype(BF16)
            key_ref[own, lanes] = (dot(grad_buf[:, own_window], queries, contract_first) * scaling).astype(BF16)
            value_ref[own, lanes] = dot(weight_buf[:, own_window], grads, contract_first).astype(BF16)


def body(queries, keys, values, out_grad, tile_image, pad_count):
    seq_index = lax.axis_index("seq")
    seq_size, tp_size = lax.axis_size("seq"), lax.axis_size("tp")
    chunk, width = queries.shape
    lanes = width // tp_size
    row_count = chunk * tp_size
    vmem = pl.BlockSpec(memory_space=pltpu.VMEM)
    doubled = pl.pallas_call(
        pack_kernel,
        out_shape=jax.ShapeDtypeStruct((2 * tp_size, 4, chunk, lanes), BF16),
        in_specs=[vmem] * 4,
        out_specs=vmem,
    )(queries, keys, values, out_grad)
    groups = [
        [seq % seq_size * tp_size + tp for seq in (left, left + 1) for tp in range(tp_size)]
        for left in range(1, seq_size, 2)
    ]
    pair = lax.all_to_all(
        doubled, ("seq", "tp"), split_axis=0, concat_axis=0, tiled=True, axis_index_groups=groups
    )
    is_right = 1 - seq_index % 2
    own = lax.dynamic_slice_in_dim(pair, is_right * tp_size, tp_size, 0)
    swaps = [(left, left + 1) for left in range(0, seq_size, 2)]
    near = lax.ppermute(own, "seq", swaps + [(right, left) for left, right in swaps])
    out = jax.ShapeDtypeStruct((row_count, lanes), BF16)
    return pl.pallas_call(
        attention_kernel,
        out_shape=[out] * 4,
        in_specs=[
            pl.BlockSpec(memory_space=pltpu.SMEM),
            pl.BlockSpec(memory_space=pltpu.SMEM),
            pl.BlockSpec(memory_space=pl.ANY),
            pl.BlockSpec(memory_space=pl.ANY),
        ],
        out_specs=[vmem] * 4,
        scratch_shapes=[
            pltpu.VMEM((3 * tp_size, 4, chunk, lanes), BF16),
            pltpu.VMEM((WINDOW * TILE, WINDOW * TILE), BF16),
            pltpu.VMEM((WINDOW * TILE, WINDOW * TILE), BF16),
            pltpu.SemaphoreType.DMA((2,)),
        ],
        compiler_params=pltpu.CompilerParams(vmem_limit_bytes=32 * 1024 * 1024),
    )(tile_image, pad_count, near, pair)


def solution(mesh):
    rows = P(("seq", "tp"), None)
    out = P("seq", "tp")
    return jax.shard_map(
        body, mesh=mesh, in_specs=(rows,) * 4 + (P(), P()), out_specs=(out,) * 4, check_vma=False
    )
```

```python
import jax
import jax.numpy as jnp
from jax import lax
from jax.experimental import pallas as pl
from jax.experimental.pallas import tpu as pltpu
from jax.sharding import PartitionSpec as P

HEAD_DIM = 128
TILE = 128
WINDOW = 3
LOG2_E = 1.4426950408889634
BF16 = jnp.bfloat16
F32 = jnp.float32


def pack_kernel(queries_ref, keys_ref, values_ref, grads_ref, packed_ref, rows, in_sems, out_sem):
    count = packed_ref.shape[0] // 2
    lanes = packed_ref.shape[3]
    sources = (queries_ref, keys_ref, values_ref, grads_ref)
    loads = [pltpu.make_async_copy(source, rows.at[index], in_sems.at[index]) for index, source in enumerate(sources)]
    for load in loads:
        load.start()
    for index, load in enumerate(loads):
        load.wait()
        for place in range(2 * count):
            block = rows.at[index, :, pl.ds(place % count * lanes, lanes)]
            pltpu.make_async_copy(block, packed_ref.at[place, index], out_sem).start()
    pltpu.make_async_copy(packed_ref, packed_ref, out_sem).wait()


def image_window(tile_image_ref, pad_count_ref, place):
    last = tile_image_ref.shape[0] - 1
    image = tile_image_ref[place]

    def same(step):
        inside = (place + step >= 0) & (place + step <= last)
        return (inside & (tile_image_ref[jnp.clip(place + step, 0, last)] == image)).astype(jnp.int32)

    back = same(-1) + same(-2)
    return back, (back + 1 + same(1) + same(2)) * TILE - pad_count_ref[image]


def attention_kernel(
    tile_image_ref,
    pad_count_ref,
    near_ref,
    pair_ref,
    attended_ref,
    query_ref,
    key_ref,
    value_ref,
    rows,
    weight_buf,
    grad_buf,
    sems,
):
    heads = attended_ref.shape[1] // HEAD_DIM
    tile_count = attended_ref.shape[0] // TILE
    near_chunks, pair_chunks = near_ref.shape[0], pair_ref.shape[0]
    chunk = near_ref.shape[2]
    per_tile = TILE // chunk
    scaling = HEAD_DIM ** (-0.5)
    seq_index = lax.axis_index("seq")
    is_right = 1 - lax.rem(seq_index, 2)
    near_at, pair_at = is_right * pair_chunks, (1 - is_right) * near_chunks
    copies = (
        pltpu.make_async_copy(pair_ref, rows.at[pl.ds(pair_at, pair_chunks)], sems.at[0]),
        pltpu.make_async_copy(near_ref, rows.at[pl.ds(near_at, near_chunks)], sems.at[1]),
    )
    for copy in copies:
        copy.start()
    windows = []
    for tile in range(tile_count):
        back, live = image_window(tile_image_ref, pad_count_ref, seq_index * tile_count + tile)
        windows.append((tile_count + tile - back, back, live))
    for copy in copies:
        copy.wait()
    contract_last = (((1,), (1,)), ((), ()))
    contract_first = (((0,), (0,)), ((), ()))

    def dot(left, right, dims):
        return lax.dot_general(left, right, dims, preferred_element_type=F32)

    key_row = lax.broadcasted_iota(jnp.int32, (WINDOW * TILE, TILE), 0)
    query_lane = lax.broadcasted_iota(jnp.int32, (1, TILE), 1)

    def place(item):
        head, tile = divmod(item, tile_count)
        start, back, live = windows[tile]
        lanes = slice(head * HEAD_DIM, (head + 1) * HEAD_DIM)
        slab = pl.ds(start * per_tile, WINDOW * per_tile)
        parts = [rows[slab, index, :, lanes].reshape(WINDOW * TILE, HEAD_DIM) for index in range(4)]
        return tile, back, live, lanes, parts, item % 2

    def weigh(item):
        _, _, live, _, (queries, keys, values, grads), slot = place(item)
        for step in range(WINDOW):
            across = slice(step * TILE, (step + 1) * TILE)
            scores = jnp.where(key_row < live, dot(keys, queries[across], contract_last), -1e30)
            value_score = dot(values, grads[across], contract_last)
            top = jnp.max(scores, axis=0, keepdims=True)
            raised = jnp.exp2((scores - top) * (scaling * LOG2_E))
            total = jnp.sum(raised, axis=0, keepdims=True)
            weights = raised * jnp.where(query_lane + step * TILE < live, 1.0 / total, 0.0)
            grad_dot = jnp.sum(weights * value_score, axis=0, keepdims=True)
            weight_buf[slot, :, across] = weights.astype(BF16)
            grad_buf[slot, :, across] = (weights * (value_score - grad_dot)).astype(BF16)

    def collect(item):
        tile, back, _, lanes, (queries, keys, values, grads), slot = place(item)
        own = slice(tile * TILE, (tile + 1) * TILE)
        inside = pl.ds(pl.multiple_of(back * TILE, TILE), TILE)
        attended_ref[own, lanes] = dot(weight_buf[slot, :, inside], values, contract_first).astype(BF16)
        query_ref[own, lanes] = (dot(grad_buf[slot, :, inside], keys, contract_first) * scaling).astype(BF16)
        key_sum = jnp.dot(grad_buf[slot, inside, :], queries, preferred_element_type=F32)
        key_ref[own, lanes] = (key_sum * scaling).astype(BF16)
        value_sum = jnp.dot(weight_buf[slot, inside, :], grads, preferred_element_type=F32)
        value_ref[own, lanes] = value_sum.astype(BF16)

    items = heads * tile_count
    for item in range(items + 1):
        if item < items:
            weigh(item)
        if item > 0:
            collect(item - 1)


def body(queries, keys, values, out_grad, tile_image, pad_count):
    seq_index = lax.axis_index("seq")
    seq_size, tp_size = lax.axis_size("seq"), lax.axis_size("tp")
    chunk, width = queries.shape
    lanes = width // tp_size
    row_count = chunk * tp_size
    vmem = pl.BlockSpec(memory_space=pltpu.VMEM)
    anywhere = pl.BlockSpec(memory_space=pl.ANY)
    doubled = pl.pallas_call(
        pack_kernel,
        out_shape=jax.ShapeDtypeStruct((2 * tp_size, 4, chunk, lanes), BF16),
        in_specs=[anywhere] * 4,
        out_specs=anywhere,
        scratch_shapes=[
            pltpu.VMEM((4, chunk, width), BF16),
            pltpu.SemaphoreType.DMA((4,)),
            pltpu.SemaphoreType.DMA,
        ],
    )(queries, keys, values, out_grad)
    groups = [
        [seq % seq_size * tp_size + tp for seq in (left, left + 1) for tp in range(tp_size)]
        for left in range(1, seq_size, 2)
    ]
    pair = lax.all_to_all(
        doubled, ("seq", "tp"), split_axis=0, concat_axis=0, tiled=True, axis_index_groups=groups
    )
    is_right = 1 - seq_index % 2
    own = lax.dynamic_slice_in_dim(pair, is_right * tp_size, tp_size, 0)
    swaps = [(left, left + 1) for left in range(0, seq_size, 2)]
    near = lax.ppermute(own, "seq", swaps + [(right, left) for left, right in swaps])
    out = jax.ShapeDtypeStruct((row_count, lanes), BF16)
    return pl.pallas_call(
        attention_kernel,
        out_shape=[out] * 4,
        in_specs=[
            pl.BlockSpec(memory_space=pltpu.SMEM),
            pl.BlockSpec(memory_space=pltpu.SMEM),
            anywhere,
            anywhere,
        ],
        out_specs=[vmem] * 4,
        scratch_shapes=[
            pltpu.VMEM((3 * tp_size, 4, chunk, lanes), BF16),
            pltpu.VMEM((2, WINDOW * TILE, WINDOW * TILE), BF16),
            pltpu.VMEM((2, WINDOW * TILE, WINDOW * TILE), BF16),
            pltpu.SemaphoreType.DMA((2,)),
        ],
        compiler_params=pltpu.CompilerParams(vmem_limit_bytes=32 * 1024 * 1024),
    )(tile_image, pad_count, near, pair)


def solution(mesh):
    rows = P(("seq", "tp"), None)
    out = P("seq", "tp")
    return jax.shard_map(
        body, mesh=mesh, in_specs=(rows,) * 4 + (P(), P()), out_specs=(out,) * 4, check_vma=False
    )
```

```python
import jax
import jax.numpy as jnp
from jax import lax
from jax.experimental import pallas as pl
from jax.experimental.pallas import tpu as pltpu
from jax.sharding import PartitionSpec as P

HEAD_DIM = 128
TILE = 128
WINDOW = 3
LOG2_E = 1.4426950408889634
BF16 = jnp.bfloat16
F32 = jnp.float32


def pack_kernel(
    tile_image_ref, queries_ref, keys_ref, values_ref, grads_ref, packed_ref, shared_ref, rows, in_sems, out_sem
):
    count = packed_ref.shape[0] // 2
    lanes = packed_ref.shape[3]
    sources = (queries_ref, keys_ref, values_ref, grads_ref)
    loads = [pltpu.make_async_copy(source, rows.at[index], in_sems.at[index]) for index, source in enumerate(sources)]
    for load in loads:
        load.start()
    last = tile_image_ref.shape[0] - 1
    tile_count = count * queries_ref.shape[0] // TILE
    seq_index = lax.axis_index("seq")
    after = (seq_index + lax.rem(seq_index, 2)) * tile_count
    joined = tile_image_ref[jnp.clip(after - 1, 0, last)] == tile_image_ref[jnp.clip(after, 0, last)]
    shared_ref[0] = ((after > 0) & (after <= last) & joined).astype(jnp.int32)
    for index, load in enumerate(loads):
        load.wait()
        for place in range(2 * count):
            block = rows.at[index, :, pl.ds(place % count * lanes, lanes)]
            pltpu.make_async_copy(block, packed_ref.at[place, index], out_sem).start()
    pltpu.make_async_copy(packed_ref, packed_ref, out_sem).wait()


def image_window(tile_image_ref, pad_count_ref, place):
    last = tile_image_ref.shape[0] - 1
    image = tile_image_ref[place]

    def same(step):
        inside = (place + step >= 0) & (place + step <= last)
        return (inside & (tile_image_ref[jnp.clip(place + step, 0, last)] == image)).astype(jnp.int32)

    back = same(-1) + same(-2)
    return back, (back + 1 + same(1) + same(2)) * TILE - pad_count_ref[image]


def attention_kernel(
    tile_image_ref,
    pad_count_ref,
    near_ref,
    pair_ref,
    attended_ref,
    query_ref,
    key_ref,
    value_ref,
    rows,
    weight_buf,
    grad_buf,
    sems,
):
    heads = attended_ref.shape[1] // HEAD_DIM
    tile_count = attended_ref.shape[0] // TILE
    near_chunks, pair_chunks = near_ref.shape[0], pair_ref.shape[0]
    chunk = near_ref.shape[2]
    per_tile = TILE // chunk
    scaling = HEAD_DIM ** (-0.5)
    seq_index = lax.axis_index("seq")
    is_right = 1 - lax.rem(seq_index, 2)
    near_at, pair_at = is_right * pair_chunks, (1 - is_right) * near_chunks
    copies = (
        pltpu.make_async_copy(pair_ref, rows.at[pl.ds(pair_at, pair_chunks)], sems.at[0]),
        pltpu.make_async_copy(near_ref, rows.at[pl.ds(near_at, near_chunks)], sems.at[1]),
    )
    for copy in copies:
        copy.start()
    windows = []
    for tile in range(tile_count):
        back, live = image_window(tile_image_ref, pad_count_ref, seq_index * tile_count + tile)
        windows.append((tile_count + tile - back, back, live))
    for copy in copies:
        copy.wait()
    contract_last = (((1,), (1,)), ((), ()))
    contract_first = (((0,), (0,)), ((), ()))

    def dot(left, right, dims):
        return lax.dot_general(left, right, dims, preferred_element_type=F32)

    key_row = lax.broadcasted_iota(jnp.int32, (WINDOW * TILE, TILE), 0)
    query_lane = lax.broadcasted_iota(jnp.int32, (1, TILE), 1)

    def place(item):
        head, tile = divmod(item, tile_count)
        start, back, live = windows[tile]
        lanes = slice(head * HEAD_DIM, (head + 1) * HEAD_DIM)
        slab = pl.ds(start * per_tile, WINDOW * per_tile)
        parts = [rows[slab, index, :, lanes].reshape(WINDOW * TILE, HEAD_DIM) for index in range(4)]
        return tile, back, live, lanes, parts, item % 2

    def weigh(item):
        _, _, live, _, (queries, keys, values, grads), slot = place(item)
        for step in range(WINDOW):
            across = slice(step * TILE, (step + 1) * TILE)
            scores = jnp.where(key_row < live, dot(keys, queries[across], contract_last), -1e30)
            value_score = dot(values, grads[across], contract_last)
            top = jnp.max(scores, axis=0, keepdims=True)
            raised = jnp.exp2((scores - top) * (scaling * LOG2_E))
            total = jnp.sum(raised, axis=0, keepdims=True)
            weights = raised * jnp.where(query_lane + step * TILE < live, 1.0 / total, 0.0)
            grad_dot = jnp.sum(weights * value_score, axis=0, keepdims=True)
            weight_buf[slot, :, across] = weights.astype(BF16)
            grad_buf[slot, :, across] = (weights * (value_score - grad_dot)).astype(BF16)

    def collect(item):
        tile, back, _, lanes, (queries, keys, values, grads), slot = place(item)
        own = slice(tile * TILE, (tile + 1) * TILE)
        inside = pl.ds(pl.multiple_of(back * TILE, TILE), TILE)
        attended_ref[own, lanes] = dot(weight_buf[slot, :, inside], values, contract_first).astype(BF16)
        query_ref[own, lanes] = (dot(grad_buf[slot, :, inside], keys, contract_first) * scaling).astype(BF16)
        key_sum = jnp.dot(grad_buf[slot, inside, :], queries, preferred_element_type=F32)
        key_ref[own, lanes] = (key_sum * scaling).astype(BF16)
        value_sum = jnp.dot(weight_buf[slot, inside, :], grads, preferred_element_type=F32)
        value_ref[own, lanes] = value_sum.astype(BF16)

    items = heads * tile_count
    for item in range(items + 1):
        if item < items:
            weigh(item)
        if item > 0:
            collect(item - 1)


def body(queries, keys, values, out_grad, tile_image, pad_count):
    seq_index = lax.axis_index("seq")
    seq_size, tp_size = lax.axis_size("seq"), lax.axis_size("tp")
    chunk, width = queries.shape
    lanes = width // tp_size
    row_count = chunk * tp_size
    vmem = pl.BlockSpec(memory_space=pltpu.VMEM)
    smem = pl.BlockSpec(memory_space=pltpu.SMEM)
    anywhere = pl.BlockSpec(memory_space=pl.ANY)
    doubled, shared = pl.pallas_call(
        pack_kernel,
        out_shape=[
            jax.ShapeDtypeStruct((2 * tp_size, 4, chunk, lanes), BF16),
            jax.ShapeDtypeStruct((1,), jnp.int32),
        ],
        in_specs=[smem] + [anywhere] * 4,
        out_specs=[anywhere, smem],
        scratch_shapes=[
            pltpu.VMEM((4, chunk, width), BF16),
            pltpu.SemaphoreType.DMA((4,)),
            pltpu.SemaphoreType.DMA,
        ],
    )(tile_image, queries, keys, values, out_grad)
    groups = [
        [seq % seq_size * tp_size + tp for seq in (left, left + 1) for tp in range(tp_size)]
        for left in range(1, seq_size, 2)
    ]

    def with_far(chunks):
        return lax.all_to_all(
            chunks, ("seq", "tp"), split_axis=0, concat_axis=0, tiled=True, axis_index_groups=groups
        )

    def own_only(chunks):
        mine = lax.all_to_all(chunks[:tp_size], "tp", split_axis=0, concat_axis=0, tiled=True)
        return jnp.concatenate([mine, mine])

    pair = lax.cond(shared[0] > 0, with_far, own_only, doubled)
    is_right = 1 - seq_index % 2
    own = lax.dynamic_slice_in_dim(pair, is_right * tp_size, tp_size, 0)
    swaps = [(left, left + 1) for left in range(0, seq_size, 2)]
    near = lax.ppermute(own, "seq", swaps + [(right, left) for left, right in swaps])
    out = jax.ShapeDtypeStruct((row_count, lanes), BF16)
    return pl.pallas_call(
        attention_kernel,
        out_shape=[out] * 4,
        in_specs=[
            smem,
            smem,
            anywhere,
            anywhere,
        ],
        out_specs=[vmem] * 4,
        scratch_shapes=[
            pltpu.VMEM((3 * tp_size, 4, chunk, lanes), BF16),
            pltpu.VMEM((2, WINDOW * TILE, WINDOW * TILE), BF16),
            pltpu.VMEM((2, WINDOW * TILE, WINDOW * TILE), BF16),
            pltpu.SemaphoreType.DMA((2,)),
        ],
        compiler_params=pltpu.CompilerParams(vmem_limit_bytes=32 * 1024 * 1024),
    )(tile_image, pad_count, near, pair)


def solution(mesh):
    rows = P(("seq", "tp"), None)
    out = P("seq", "tp")
    return jax.shard_map(
        body, mesh=mesh, in_specs=(rows,) * 4 + (P(), P()), out_specs=(out,) * 4, check_vma=False
    )
```

```python
import jax
import jax.numpy as jnp
from jax import lax
from jax.experimental import pallas as pl
from jax.experimental.pallas import tpu as pltpu
from jax.sharding import PartitionSpec as P

HEAD_DIM = 128
TILE = 128
WINDOW = 3
LOG2_E = 1.4426950408889634
BF16 = jnp.bfloat16
F32 = jnp.float32


def pack_kernel(
    tile_image_ref,
    queries_ref,
    keys_ref,
    values_ref,
    grads_ref,
    packed_ref,
    shared_ref,
    rows,
    images,
    shared,
    in_sems,
    out_sem,
    scalar_sems,
):
    count = packed_ref.shape[0] // 2
    lanes = packed_ref.shape[3]
    sources = (queries_ref, keys_ref, values_ref, grads_ref)
    fetch = pltpu.make_async_copy(tile_image_ref, images, scalar_sems.at[0])
    fetch.start()
    loads = [pltpu.make_async_copy(source, rows.at[index], in_sems.at[index]) for index, source in enumerate(sources)]
    for load in loads:
        load.start()
    last = tile_image_ref.shape[0] - 1
    tile_count = count * queries_ref.shape[0] // TILE
    seq_index = lax.axis_index("seq")
    after = (seq_index + lax.rem(seq_index, 2)) * tile_count
    fetch.wait()
    joined = images[jnp.clip(after - 1, 0, last)] == images[jnp.clip(after, 0, last)]
    shared[0] = ((after > 0) & (after <= last) & joined).astype(jnp.int32)
    tell = pltpu.make_async_copy(shared, shared_ref, scalar_sems.at[1])
    tell.start()
    for index, load in enumerate(loads):
        load.wait()
        for place in range(2 * count):
            block = rows.at[index, :, pl.ds(place % count * lanes, lanes)]
            pltpu.make_async_copy(block, packed_ref.at[place, index], out_sem).start()
    pltpu.make_async_copy(packed_ref, packed_ref, out_sem).wait()
    tell.wait()


def image_window(tile_image_ref, pad_count_ref, place):
    last = tile_image_ref.shape[0] - 1
    image = tile_image_ref[place]

    def same(step):
        inside = (place + step >= 0) & (place + step <= last)
        return (inside & (tile_image_ref[jnp.clip(place + step, 0, last)] == image)).astype(jnp.int32)

    back = same(-1) + same(-2)
    return back, (back + 1 + same(1) + same(2)) * TILE - pad_count_ref[image]


def dot(left, right, dims):
    return lax.dot_general(left, right, dims, preferred_element_type=F32)


def attend(heads, load, first_live, live, weight_buf, grad_buf, stores):
    scaling = HEAD_DIM ** (-0.5)
    contract_last = (((1,), (1,)), ((), ()))
    contract_first = (((0,), (0,)), ((), ()))
    key_row = lax.broadcasted_iota(jnp.int32, (WINDOW * TILE, TILE), 0)
    query_lane = lax.broadcasted_iota(jnp.int32, (1, TILE), 1)

    def inside(places):
        return (places >= first_live) & (places < first_live + live)

    def weigh(head):
        queries, keys, values, grads = load(head)
        for step in range(WINDOW):
            across = slice(step * TILE, (step + 1) * TILE)
            scores = jnp.where(inside(key_row), dot(keys, queries[across], contract_last), -1e30)
            value_score = dot(values, grads[across], contract_last)
            top = jnp.max(scores, axis=0, keepdims=True)
            raised = jnp.exp2((scores - top) * (scaling * LOG2_E))
            total = jnp.sum(raised, axis=0, keepdims=True)
            weights = raised * jnp.where(inside(query_lane + step * TILE), 1.0 / total, 0.0)
            grad_dot = jnp.sum(weights * value_score, axis=0, keepdims=True)
            weight_buf[head, :, across] = weights.astype(BF16)
            grad_buf[head, :, across] = (weights * (value_score - grad_dot)).astype(BF16)

    def collect(head, at, store):
        queries, keys, values, grads = load(head)
        own = pl.ds(pl.multiple_of(at * TILE, TILE), TILE)
        attended = dot(weight_buf[head, :, own], values, contract_first)
        query_sum = dot(grad_buf[head, :, own], keys, contract_first)
        key_sum = jnp.dot(grad_buf[head, own, :], queries, preferred_element_type=F32)
        value_sum = jnp.dot(weight_buf[head, own, :], grads, preferred_element_type=F32)
        results = (attended, query_sum * scaling, key_sum * scaling, value_sum)
        store(head, [result.astype(BF16) for result in results])

    (at, store), *others = stores
    for head in range(heads + 1):
        if head < heads:
            weigh(head)
        if head > 0:
            collect(head - 1, at, store)
    for wanted, at, store in others:

        @pl.when(wanted)
        def _():
            for head in range(heads):
                collect(head, at, store)


def head_lanes(head):
    return slice(head * HEAD_DIM, (head + 1) * HEAD_DIM)


def near_tile(is_right):
    return is_right, 3 * is_right - 1


def spans_near(tile_image_ref, first_tile, is_right):
    last = tile_image_ref.shape[0] - 1
    mine, beyond = near_tile(is_right)
    beyond = first_tile + beyond
    same = tile_image_ref[first_tile + mine] == tile_image_ref[jnp.clip(beyond, 0, last)]
    return (beyond >= 0) & (beyond <= last) & same


def far_kernel(
    tile_image_ref, pad_count_ref, pair_ref, attended_ref, query_ref, key_ref, value_ref, weight_buf, grad_buf
):
    heads = attended_ref.shape[1] // HEAD_DIM
    tile_count = attended_ref.shape[0] // TILE
    per_tile = TILE // pair_ref.shape[2]
    seq_index = lax.axis_index("seq")
    is_right = 1 - lax.rem(seq_index, 2)
    first_tile = seq_index * tile_count
    near_image = tile_image_ref[first_tile + near_tile(is_right)[0]]
    spans = spans_near(tile_image_ref, first_tile, is_right)
    outs = (attended_ref, query_ref, key_ref, value_ref)
    for tile in range(tile_count):
        back, live = image_window(tile_image_ref, pad_count_ref, first_tile + tile)
        place = tile_count * is_right + tile
        start = jnp.minimum(place - back, 1)

        def load(head):
            slab = pl.ds(start * per_tile, WINDOW * per_tile)
            lanes = head_lanes(head)
            return [pair_ref[slab, index, :, lanes].reshape(WINDOW * TILE, HEAD_DIM) for index in range(4)]

        def store(head, results):
            for out, result in zip(outs, results):
                out[tile * TILE : (tile + 1) * TILE, head_lanes(head)] = result

        @pl.when(jnp.logical_not(spans & (tile_image_ref[first_tile + tile] == near_image)))
        def _():
            first_live = (place - back - start) * TILE
            attend(heads, load, first_live, live, weight_buf, grad_buf, [(place - start, store)])


def near_kernel(
    tile_image_ref,
    pad_count_ref,
    near_ref,
    pair_ref,
    attended_in,
    query_in,
    key_in,
    value_in,
    attended_ref,
    query_ref,
    key_ref,
    value_ref,
    results,
    weight_buf,
    grad_buf,
    sems,
):
    del attended_in, query_in, key_in, value_in
    heads = attended_ref.shape[1] // HEAD_DIM
    tile_count = attended_ref.shape[0] // TILE
    per_tile = TILE // pair_ref.shape[2]
    seq_index = lax.axis_index("seq")
    is_right = 1 - lax.rem(seq_index, 2)
    first_tile = seq_index * tile_count
    outs = (attended_ref, query_ref, key_ref, value_ref)
    main = near_tile(is_right)[0]
    other = 1 - main
    back, live = image_window(tile_image_ref, pad_count_ref, first_tile + main)
    place = main + tile_count * (1 - is_right)
    start = place - back
    both = tile_image_ref[first_tile] == tile_image_ref[first_tile + 1]

    def load(head):
        parts = []
        for index in range(4):
            tiles = []
            for step in range(WINDOW):
                lower = start + step < tile_count
                from_near = lower == (is_right == 0)
                within = lax.rem(start + step, tile_count)
                near_slab = pl.ds(within * per_tile, per_tile)
                own_slab = pl.ds((within + tile_count * is_right) * per_tile, per_tile)
                lanes = head_lanes(head)
                tile = jnp.where(from_near, near_ref[near_slab, index, :, lanes], pair_ref[own_slab, index, :, lanes])
                tiles.append(tile.reshape(TILE, HEAD_DIM))
            parts.append(jnp.concatenate(tiles))
        return parts

    def store_at(slot):
        def store(head, values):
            for index, value in enumerate(values):
                results[slot, index, :, head_lanes(head)] = value

        return store

    def copies(slot, tile):
        rows = pl.ds(pl.multiple_of(tile * TILE, TILE), TILE)
        return [
            pltpu.make_async_copy(results.at[slot, index], out.at[rows], sems.at[slot, index])
            for index, out in enumerate(outs)
        ]

    @pl.when(spans_near(tile_image_ref, first_tile, is_right))
    def _():
        stores = [(place - start, store_at(0)), (both, place - start + other - main, store_at(1))]
        attend(heads, load, 0, live, weight_buf, grad_buf, stores)
        for copy in copies(0, main):
            copy.start()

        @pl.when(both)
        def _():
            for copy in copies(1, other):
                copy.start()
            for copy in copies(1, other):
                copy.wait()

        for copy in copies(0, main):
            copy.wait()


def body(queries, keys, values, out_grad, tile_image, pad_count):
    seq_index = lax.axis_index("seq")
    seq_size, tp_size = lax.axis_size("seq"), lax.axis_size("tp")
    chunk, width = queries.shape
    lanes = width // tp_size
    row_count = chunk * tp_size
    vmem = pl.BlockSpec(memory_space=pltpu.VMEM)
    smem = pl.BlockSpec(memory_space=pltpu.SMEM)
    anywhere = pl.BlockSpec(memory_space=pl.ANY)
    doubled, shared = pl.pallas_call(
        pack_kernel,
        out_shape=[
            jax.ShapeDtypeStruct((2 * tp_size, 4, chunk, lanes), BF16),
            jax.ShapeDtypeStruct((1,), jnp.int32),
        ],
        in_specs=[anywhere] * 5,
        out_specs=[anywhere] * 2,
        scratch_shapes=[
            pltpu.VMEM((4, chunk, width), BF16),
            pltpu.SMEM(tile_image.shape, jnp.int32),
            pltpu.SMEM((1,), jnp.int32),
            pltpu.SemaphoreType.DMA((4,)),
            pltpu.SemaphoreType.DMA,
            pltpu.SemaphoreType.DMA((2,)),
        ],
    )(tile_image, queries, keys, values, out_grad)
    groups = [
        [seq % seq_size * tp_size + tp for seq in (left, left + 1) for tp in range(tp_size)]
        for left in range(1, seq_size, 2)
    ]

    def with_far(chunks):
        return lax.all_to_all(
            chunks, ("seq", "tp"), split_axis=0, concat_axis=0, tiled=True, axis_index_groups=groups
        )

    def own_only(chunks):
        mine = lax.all_to_all(chunks[:tp_size], "tp", split_axis=0, concat_axis=0, tiled=True)
        return jnp.concatenate([mine, mine])

    pair = lax.cond(shared[0] > 0, with_far, own_only, doubled)
    is_right = 1 - seq_index % 2
    own = lax.dynamic_slice_in_dim(pair, is_right * tp_size, tp_size, 0)
    swaps = [(left, left + 1) for left in range(0, seq_size, 2)]
    near = lax.ppermute(own, "seq", swaps + [(right, left) for left, right in swaps])
    out = jax.ShapeDtypeStruct((row_count, lanes), BF16)
    heads = lanes // HEAD_DIM
    square = pltpu.VMEM((heads, WINDOW * TILE, WINDOW * TILE), BF16)
    params = pltpu.CompilerParams(vmem_limit_bytes=24 * 1024 * 1024)
    work = heads * 2 * 12 * (WINDOW * TILE) ** 2 * HEAD_DIM
    cost = pl.CostEstimate(flops=work, bytes_accessed=pair.size * 2, transcendentals=heads * 2 * (WINDOW * TILE) ** 2)
    started = pl.pallas_call(
        far_kernel,
        out_shape=[out] * 4,
        in_specs=[smem, smem, vmem],
        out_specs=[vmem] * 4,
        scratch_shapes=[square, square],
        compiler_params=params,
        cost_estimate=cost,
    )(tile_image, pad_count, pair)
    return pl.pallas_call(
        near_kernel,
        out_shape=[out] * 4,
        in_specs=[smem, smem, vmem, vmem] + [anywhere] * 4,
        out_specs=[anywhere] * 4,
        scratch_shapes=[
            pltpu.VMEM((2, 4, TILE, lanes), BF16),
            square,
            square,
            pltpu.SemaphoreType.DMA((2, 4)),
        ],
        input_output_aliases={4 + index: index for index in range(4)},
        compiler_params=params,
    )(tile_image, pad_count, near, pair, *started)


def solution(mesh):
    rows = P(("seq", "tp"), None)
    out = P("seq", "tp")
    return jax.shard_map(
        body, mesh=mesh, in_specs=(rows,) * 4 + (P(), P()), out_specs=(out,) * 4, check_vma=False
    )
```

```python
import jax
import jax.numpy as jnp
from jax import lax
from jax.experimental import pallas as pl
from jax.experimental.pallas import tpu as pltpu
from jax.sharding import PartitionSpec as P

HEAD_DIM = 128
TILE = 128
WINDOW = 3
LOG2_E = 1.4426950408889634
BF16 = jnp.bfloat16
F32 = jnp.float32


def group_order(count):
    return [place for step in range(count) for place in (step, 2 * count - 1 - step)]


def chunk_place(token_chunk, count):
    return jnp.where(token_chunk < count, 2 * token_chunk, 4 * count - 1 - 2 * token_chunk)


def pack_kernel(
    tile_image_ref,
    queries_ref,
    keys_ref,
    values_ref,
    grads_ref,
    packed_ref,
    shared_ref,
    rows,
    images,
    shared,
    in_sems,
    out_sem,
    scalar_sems,
):
    count = packed_ref.shape[0] // 2
    lanes = packed_ref.shape[3]
    sources = (queries_ref, keys_ref, values_ref, grads_ref)
    fetch = pltpu.make_async_copy(tile_image_ref, images, scalar_sems.at[0])
    fetch.start()
    loads = [pltpu.make_async_copy(source, rows.at[index], in_sems.at[index]) for index, source in enumerate(sources)]
    for load in loads:
        load.start()
    last = tile_image_ref.shape[0] - 1
    tile_count = count * queries_ref.shape[0] // TILE
    seq_index = lax.axis_index("seq")
    after = (seq_index + lax.rem(seq_index, 2)) * tile_count
    fetch.wait()
    joined = images[jnp.clip(after - 1, 0, last)] == images[jnp.clip(after, 0, last)]
    shared[0] = ((after > 0) & (after <= last) & joined).astype(jnp.int32)
    tell = pltpu.make_async_copy(shared, shared_ref, scalar_sems.at[1])
    tell.start()
    for index, load in enumerate(loads):
        load.wait()
        for place, member in enumerate(group_order(count)):
            block = rows.at[index, :, pl.ds(member % count * lanes, lanes)]
            pltpu.make_async_copy(block, packed_ref.at[place, index], out_sem).start()
    pltpu.make_async_copy(packed_ref, packed_ref, out_sem).wait()
    tell.wait()


def image_window(tile_image_ref, pad_count_ref, place):
    last = tile_image_ref.shape[0] - 1
    image = tile_image_ref[place]

    def same(step):
        inside = (place + step >= 0) & (place + step <= last)
        return (inside & (tile_image_ref[jnp.clip(place + step, 0, last)] == image)).astype(jnp.int32)

    back = same(-1) + same(-2)
    return back, (back + 1 + same(1) + same(2)) * TILE - pad_count_ref[image]


def dot(left, right, dims):
    return lax.dot_general(left, right, dims, preferred_element_type=F32)


def attend(load, live, weight_bufs, grad_bufs, stores):
    heads = len(weight_bufs)
    scaling = HEAD_DIM ** (-0.5)
    contract_last = (((1,), (1,)), ((), ()))
    contract_first = (((0,), (0,)), ((), ()))
    key_row = lax.broadcasted_iota(jnp.int32, (WINDOW * TILE, TILE), 0)
    query_lane = lax.broadcasted_iota(jnp.int32, (1, TILE), 1)

    def weigh(head):
        queries, keys, values, grads = load(head)
        for step in range(WINDOW):
            across = slice(step * TILE, (step + 1) * TILE)
            scores = jnp.where(key_row < live, dot(keys, queries[across], contract_last), -1e30)
            value_score = dot(values, grads[across], contract_last)
            top = jnp.max(scores, axis=0, keepdims=True)
            raised = jnp.exp2((scores - top) * (scaling * LOG2_E))
            total = jnp.sum(raised, axis=0, keepdims=True)
            weights = raised * jnp.where(query_lane + step * TILE < live, 1.0 / total, 0.0)
            grad_dot = jnp.sum(weights * value_score, axis=0, keepdims=True)
            weight_bufs[head][:, across] = weights.astype(BF16)
            grad_bufs[head][:, across] = (weights * (value_score - grad_dot)).astype(BF16)

    def collect(head, at, store):
        queries, keys, values, grads = load(head)
        own = pl.ds(pl.multiple_of(at * TILE, TILE), TILE)
        attended = dot(weight_bufs[head][:, own], values, contract_first)
        query_sum = dot(grad_bufs[head][:, own], keys, contract_first)
        key_sum = jnp.dot(grad_bufs[head][own, :], queries, preferred_element_type=F32)
        value_sum = jnp.dot(weight_bufs[head][own, :], grads, preferred_element_type=F32)
        results = (attended, query_sum * scaling, key_sum * scaling, value_sum)
        store(head, [result.astype(BF16) for result in results])

    (at, store), *others = stores
    for head in range(heads + 1):
        if head < heads:
            weigh(head)
        if head > 0:
            collect(head - 1, at, store)
    for wanted, at, store in others:

        @pl.when(wanted)
        def _():
            for head in range(heads):
                collect(head, at, store)


def head_lanes(head):
    return slice(head * HEAD_DIM, (head + 1) * HEAD_DIM)


def near_tile(is_right):
    return is_right, 3 * is_right - 1


def spans_near(tile_image_ref, first_tile, is_right):
    last = tile_image_ref.shape[0] - 1
    mine, beyond = near_tile(is_right)
    beyond = first_tile + beyond
    same = tile_image_ref[first_tile + mine] == tile_image_ref[jnp.clip(beyond, 0, last)]
    return (beyond >= 0) & (beyond <= last) & same


def window_load(window):
    def load(head):
        lanes = head_lanes(head)
        return [window[:, index, :, lanes].reshape(WINDOW * TILE, HEAD_DIM) for index in range(4)]

    return load


def far_kernel(
    tile_image_ref, pad_count_ref, pair_ref, attended_ref, query_ref, key_ref, value_ref, window, *bufs
):
    tile_count = attended_ref.shape[0] // TILE
    per_tile = TILE // pair_ref.shape[2]
    count = pair_ref.shape[0] // 2
    heads = len(bufs) // 2
    seq_index = lax.axis_index("seq")
    is_right = 1 - lax.rem(seq_index, 2)
    first_tile = seq_index * tile_count
    near_image = tile_image_ref[first_tile + near_tile(is_right)[0]]
    spans = spans_near(tile_image_ref, first_tile, is_right)
    outs = (attended_ref, query_ref, key_ref, value_ref)
    mine = [
        jnp.logical_not(spans & (tile_image_ref[first_tile + tile] == near_image)) for tile in range(tile_count)
    ]
    spots = [image_window(tile_image_ref, pad_count_ref, first_tile + tile) for tile in range(tile_count)]
    for tile in range(tile_count):
        start = tile_count * is_right + tile - spots[tile][0]

        def store(head, results):
            for out, result in zip(outs, results):
                out[tile * TILE : (tile + 1) * TILE, head_lanes(head)] = result

        @pl.when(mine[tile])
        def _():
            for step in range(WINDOW):
                within = lax.rem(start + step, 2 * tile_count) * per_tile
                for chunk in range(per_tile):
                    window[step * per_tile + chunk] = pair_ref[chunk_place(within + chunk, count)]
            attend(window_load(window), spots[tile][1], bufs[:heads], bufs[heads:], [(spots[tile][0], store)])


def near_kernel(
    tile_image_ref,
    pad_count_ref,
    near_ref,
    pair_ref,
    attended_in,
    query_in,
    key_in,
    value_in,
    attended_ref,
    query_ref,
    key_ref,
    value_ref,
    results,
    window,
    sems,
    *bufs,
):
    del attended_in, query_in, key_in, value_in
    tile_count = attended_ref.shape[0] // TILE
    per_tile = TILE // pair_ref.shape[2]
    count = near_ref.shape[0]
    heads = len(bufs) // 2
    seq_index = lax.axis_index("seq")
    is_right = 1 - lax.rem(seq_index, 2)
    first_tile = seq_index * tile_count
    outs = (attended_ref, query_ref, key_ref, value_ref)
    main = near_tile(is_right)[0]
    other = 1 - main
    back, live = image_window(tile_image_ref, pad_count_ref, first_tile + main)
    place = main + tile_count * (1 - is_right)
    start = place - back
    both = tile_image_ref[first_tile] == tile_image_ref[first_tile + 1]

    def gather():
        for step in range(WINDOW):
            lower = start + step < tile_count
            from_near = lower == (is_right == 0)
            within = lax.rem(start + step, tile_count) * per_tile
            near_at = [jnp.where(is_right == 1, within + chunk, count - 1 - within - chunk) for chunk in range(per_tile)]
            own_at = [chunk_place(within + chunk + count * is_right, count) for chunk in range(per_tile)]
            for wanted, source, places in ((from_near, near_ref, near_at), (~from_near, pair_ref, own_at)):

                @pl.when(wanted)
                def _():
                    for chunk in range(per_tile):
                        window[step * per_tile + chunk] = source[places[chunk]]

    def store_at(slot):
        def store(head, values):
            for index, value in enumerate(values):
                results[slot, index, :, head_lanes(head)] = value

        return store

    def copies(slot, tile):
        rows = pl.ds(pl.multiple_of(tile * TILE, TILE), TILE)
        return [
            pltpu.make_async_copy(results.at[slot, index], out.at[rows], sems.at[slot, index])
            for index, out in enumerate(outs)
        ]

    @pl.when(spans_near(tile_image_ref, first_tile, is_right))
    def _():
        stores = [(place - start, store_at(0)), (both, place - start + other - main, store_at(1))]
        gather()
        attend(window_load(window), live, bufs[:heads], bufs[heads:], stores)
        for copy in copies(0, main):
            copy.start()

        @pl.when(both)
        def _():
            for copy in copies(1, other):
                copy.start()
            for copy in copies(1, other):
                copy.wait()

        for copy in copies(0, main):
            copy.wait()


def body(queries, keys, values, out_grad, tile_image, pad_count):
    seq_index = lax.axis_index("seq")
    seq_size, tp_size = lax.axis_size("seq"), lax.axis_size("tp")
    chunk, width = queries.shape
    lanes = width // tp_size
    row_count = chunk * tp_size
    vmem = pl.BlockSpec(memory_space=pltpu.VMEM)
    smem = pl.BlockSpec(memory_space=pltpu.SMEM)
    anywhere = pl.BlockSpec(memory_space=pl.ANY)
    doubled, shared = pl.pallas_call(
        pack_kernel,
        out_shape=[
            jax.ShapeDtypeStruct((2 * tp_size, 4, chunk, lanes), BF16),
            jax.ShapeDtypeStruct((1,), jnp.int32),
        ],
        in_specs=[anywhere] * 5,
        out_specs=[anywhere] * 2,
        scratch_shapes=[
            pltpu.VMEM((4, chunk, width), BF16),
            pltpu.SMEM(tile_image.shape, jnp.int32),
            pltpu.SMEM((1,), jnp.int32),
            pltpu.SemaphoreType.DMA((4,)),
            pltpu.SemaphoreType.DMA,
            pltpu.SemaphoreType.DMA((2,)),
        ],
    )(tile_image, queries, keys, values, out_grad)
    groups = [
        [(left + place // tp_size) % seq_size * tp_size + place % tp_size for place in group_order(tp_size)]
        for left in range(1, seq_size, 2)
    ]

    def with_far(chunks):
        return lax.all_to_all(
            chunks, ("seq", "tp"), split_axis=0, concat_axis=0, tiled=True, axis_index_groups=groups
        )

    def own_only(chunks):
        mine = lax.all_to_all(chunks[::2], "tp", split_axis=0, concat_axis=0, tiled=True)
        return jnp.stack([mine, mine[::-1]], axis=1).reshape(chunks.shape)

    pair = lax.cond(shared[0] > 0, with_far, own_only, doubled)
    is_right = 1 - seq_index % 2
    own = jnp.where(is_right == 1, pair[1::2], pair[::2])
    swaps = [(left, left + 1) for left in range(0, seq_size, 2)]
    near = lax.ppermute(own, "seq", swaps + [(right, left) for left, right in swaps])
    out = jax.ShapeDtypeStruct((row_count, lanes), BF16)
    heads = lanes // HEAD_DIM
    window = pltpu.VMEM((WINDOW * TILE // chunk, 4, chunk, lanes), BF16)
    squares = [pltpu.VMEM((WINDOW * TILE, WINDOW * TILE), BF16)] * (2 * heads)
    params = pltpu.CompilerParams(vmem_limit_bytes=24 * 1024 * 1024)
    work = heads * 2 * 12 * (WINDOW * TILE) ** 2 * HEAD_DIM
    cost = pl.CostEstimate(flops=work, bytes_accessed=pair.size * 2, transcendentals=heads * 2 * (WINDOW * TILE) ** 2)
    started = pl.pallas_call(
        far_kernel,
        out_shape=[out] * 4,
        in_specs=[smem, smem, vmem],
        out_specs=[vmem] * 4,
        scratch_shapes=[window, *squares],
        compiler_params=params,
        cost_estimate=cost,
    )(tile_image, pad_count, pair)
    return pl.pallas_call(
        near_kernel,
        out_shape=[out] * 4,
        in_specs=[smem, smem, vmem, vmem] + [anywhere] * 4,
        out_specs=[anywhere] * 4,
        scratch_shapes=[
            pltpu.VMEM((2, 4, TILE, lanes), BF16),
            window,
            pltpu.SemaphoreType.DMA((2, 4)),
            *squares,
        ],
        input_output_aliases={4 + index: index for index in range(4)},
        compiler_params=params,
    )(tile_image, pad_count, near, pair, *started)


def solution(mesh):
    rows = P(("seq", "tp"), None)
    out = P("seq", "tp")
    return jax.shard_map(
        body, mesh=mesh, in_specs=(rows,) * 4 + (P(), P()), out_specs=(out,) * 4, check_vma=False
    )
```

```python
import jax
import jax.numpy as jnp
from jax import lax
from jax.experimental import pallas as pl
from jax.experimental.pallas import tpu as pltpu
from jax.sharding import PartitionSpec as P

HEAD_DIM = 128
TILE = 128
WINDOW = 3
LOG2_E = 1.4426950408889634
BF16 = jnp.bfloat16
F32 = jnp.float32


def group_order(count):
    return [place for step in range(count) for place in (step, count + step)]


def chunk_place(token_chunk, count):
    return jnp.where(token_chunk < count, 2 * token_chunk, 2 * (token_chunk - count) + 1)


def pack_kernel(
    tile_image_ref,
    queries_ref,
    keys_ref,
    values_ref,
    grads_ref,
    packed_ref,
    shared_ref,
    rows,
    images,
    shared,
    in_sems,
    out_sem,
    scalar_sems,
):
    count = packed_ref.shape[0] // 2
    lanes = packed_ref.shape[3]
    sources = (queries_ref, keys_ref, values_ref, grads_ref)
    fetch = pltpu.make_async_copy(tile_image_ref, images, scalar_sems.at[0])
    fetch.start()
    loads = [pltpu.make_async_copy(source, rows.at[index], in_sems.at[index]) for index, source in enumerate(sources)]
    for load in loads:
        load.start()
    last = tile_image_ref.shape[0] - 1
    tile_count = count * queries_ref.shape[0] // TILE
    seq_index = lax.axis_index("seq")
    after = (seq_index + lax.rem(seq_index, 2)) * tile_count
    fetch.wait()
    joined = images[jnp.clip(after - 1, 0, last)] == images[jnp.clip(after, 0, last)]
    shared[0] = ((after > 0) & (after <= last) & joined).astype(jnp.int32)
    tell = pltpu.make_async_copy(shared, shared_ref, scalar_sems.at[1])
    tell.start()
    for index, load in enumerate(loads):
        load.wait()
        for place, member in enumerate(group_order(count)):
            block = rows.at[index, :, pl.ds(member % count * lanes, lanes)]
            pltpu.make_async_copy(block, packed_ref.at[place, index], out_sem).start()
    pltpu.make_async_copy(packed_ref, packed_ref, out_sem).wait()
    tell.wait()


def image_window(tile_image_ref, pad_count_ref, place):
    last = tile_image_ref.shape[0] - 1
    image = tile_image_ref[place]

    def same(step):
        inside = (place + step >= 0) & (place + step <= last)
        return (inside & (tile_image_ref[jnp.clip(place + step, 0, last)] == image)).astype(jnp.int32)

    back = same(-1) + same(-2)
    return back, (back + 1 + same(1) + same(2)) * TILE - pad_count_ref[image]


def dot(left, right, dims):
    return lax.dot_general(left, right, dims, preferred_element_type=F32)


def attend(load, live, weight_bufs, grad_bufs, stores):
    heads = len(weight_bufs)
    scaling = HEAD_DIM ** (-0.5)
    contract_last = (((1,), (1,)), ((), ()))
    contract_first = (((0,), (0,)), ((), ()))
    key_row = lax.broadcasted_iota(jnp.int32, (WINDOW * TILE, TILE), 0)
    query_lane = lax.broadcasted_iota(jnp.int32, (1, TILE), 1)

    def weigh(head):
        queries, keys, values, grads = load(head)
        for step in range(WINDOW):
            across = slice(step * TILE, (step + 1) * TILE)
            scores = jnp.where(key_row < live, dot(keys, queries[across], contract_last), -1e30)
            value_score = dot(values, grads[across], contract_last)
            top = jnp.max(scores, axis=0, keepdims=True)
            raised = jnp.exp2((scores - top) * (scaling * LOG2_E))
            total = jnp.sum(raised, axis=0, keepdims=True)
            weights = raised * jnp.where(query_lane + step * TILE < live, 1.0 / total, 0.0)
            grad_dot = jnp.sum(weights * value_score, axis=0, keepdims=True)
            weight_bufs[head][:, across] = weights.astype(BF16)
            grad_bufs[head][:, across] = (weights * (value_score - grad_dot)).astype(BF16)

    def collect(head, at, store):
        queries, keys, values, grads = load(head)
        own = pl.ds(pl.multiple_of(at * TILE, TILE), TILE)
        attended = dot(weight_bufs[head][:, own], values, contract_first)
        query_sum = dot(grad_bufs[head][:, own], keys, contract_first)
        key_sum = jnp.dot(grad_bufs[head][own, :], queries, preferred_element_type=F32)
        value_sum = jnp.dot(weight_bufs[head][own, :], grads, preferred_element_type=F32)
        results = (attended, query_sum * scaling, key_sum * scaling, value_sum)
        store(head, [result.astype(BF16) for result in results])

    (at, store), *others = stores
    for head in range(heads + 1):
        if head < heads:
            weigh(head)
        if head > 0:
            collect(head - 1, at, store)
    for wanted, at, store in others:

        @pl.when(wanted)
        def _():
            for head in range(heads):
                collect(head, at, store)


def head_lanes(head):
    return slice(head * HEAD_DIM, (head + 1) * HEAD_DIM)


def near_tile(is_right):
    return is_right, 3 * is_right - 1


def spans_near(tile_image_ref, first_tile, is_right):
    last = tile_image_ref.shape[0] - 1
    mine, beyond = near_tile(is_right)
    beyond = first_tile + beyond
    same = tile_image_ref[first_tile + mine] == tile_image_ref[jnp.clip(beyond, 0, last)]
    return (beyond >= 0) & (beyond <= last) & same


def window_load(window):
    def load(head):
        lanes = head_lanes(head)
        return [window[:, index, :, lanes].reshape(WINDOW * TILE, HEAD_DIM) for index in range(4)]

    return load


def far_kernel(
    tile_image_ref, pad_count_ref, pair_ref, attended_ref, query_ref, key_ref, value_ref, window, *bufs
):
    tile_count = attended_ref.shape[0] // TILE
    per_tile = TILE // pair_ref.shape[2]
    count = pair_ref.shape[0] // 2
    heads = len(bufs) // 2
    seq_index = lax.axis_index("seq")
    is_right = 1 - lax.rem(seq_index, 2)
    first_tile = seq_index * tile_count
    near_image = tile_image_ref[first_tile + near_tile(is_right)[0]]
    spans = spans_near(tile_image_ref, first_tile, is_right)
    outs = (attended_ref, query_ref, key_ref, value_ref)
    mine = [
        jnp.logical_not(spans & (tile_image_ref[first_tile + tile] == near_image)) for tile in range(tile_count)
    ]
    spots = [image_window(tile_image_ref, pad_count_ref, first_tile + tile) for tile in range(tile_count)]
    for tile in range(tile_count):
        start = tile_count * is_right + tile - spots[tile][0]

        def store(head, results):
            for out, result in zip(outs, results):
                out[tile * TILE : (tile + 1) * TILE, head_lanes(head)] = result

        @pl.when(mine[tile])
        def _():
            for step in range(WINDOW):
                within = lax.rem(start + step, 2 * tile_count) * per_tile
                for chunk in range(per_tile):
                    window[step * per_tile + chunk] = pair_ref[chunk_place(within + chunk, count)]
            attend(window_load(window), spots[tile][1], bufs[:heads], bufs[heads:], [(spots[tile][0], store)])


def near_kernel(
    tile_image_ref,
    pad_count_ref,
    near_ref,
    pair_ref,
    attended_in,
    query_in,
    key_in,
    value_in,
    attended_ref,
    query_ref,
    key_ref,
    value_ref,
    results,
    window,
    sems,
    *bufs,
):
    del attended_in, query_in, key_in, value_in
    tile_count = attended_ref.shape[0] // TILE
    per_tile = TILE // pair_ref.shape[2]
    count = near_ref.shape[0]
    heads = len(bufs) // 2
    seq_index = lax.axis_index("seq")
    is_right = 1 - lax.rem(seq_index, 2)
    first_tile = seq_index * tile_count
    outs = (attended_ref, query_ref, key_ref, value_ref)
    main = near_tile(is_right)[0]
    other = 1 - main
    back, live = image_window(tile_image_ref, pad_count_ref, first_tile + main)
    place = main + tile_count * (1 - is_right)
    start = place - back
    both = tile_image_ref[first_tile] == tile_image_ref[first_tile + 1]

    def gather():
        for step in range(WINDOW):
            lower = start + step < tile_count
            from_near = lower == (is_right == 0)
            within = lax.rem(start + step, tile_count) * per_tile
            near_at = [within + chunk for chunk in range(per_tile)]
            own_at = [chunk_place(within + chunk + count * is_right, count) for chunk in range(per_tile)]
            for wanted, source, places in ((from_near, near_ref, near_at), (~from_near, pair_ref, own_at)):

                @pl.when(wanted)
                def _():
                    for chunk in range(per_tile):
                        window[step * per_tile + chunk] = source[places[chunk]]

    def store_at(slot):
        def store(head, values):
            for index, value in enumerate(values):
                results[slot, index, :, head_lanes(head)] = value

        return store

    def copies(slot, tile):
        rows = pl.ds(pl.multiple_of(tile * TILE, TILE), TILE)
        return [
            pltpu.make_async_copy(results.at[slot, index], out.at[rows], sems.at[slot, index])
            for index, out in enumerate(outs)
        ]

    @pl.when(spans_near(tile_image_ref, first_tile, is_right))
    def _():
        stores = [(place - start, store_at(0)), (both, place - start + other - main, store_at(1))]
        gather()
        attend(window_load(window), live, bufs[:heads], bufs[heads:], stores)
        for copy in copies(0, main):
            copy.start()

        @pl.when(both)
        def _():
            for copy in copies(1, other):
                copy.start()
            for copy in copies(1, other):
                copy.wait()

        for copy in copies(0, main):
            copy.wait()


def body(queries, keys, values, out_grad, tile_image, pad_count):
    seq_index = lax.axis_index("seq")
    seq_size, tp_size = lax.axis_size("seq"), lax.axis_size("tp")
    chunk, width = queries.shape
    lanes = width // tp_size
    row_count = chunk * tp_size
    vmem = pl.BlockSpec(memory_space=pltpu.VMEM)
    smem = pl.BlockSpec(memory_space=pltpu.SMEM)
    anywhere = pl.BlockSpec(memory_space=pl.ANY)
    doubled, shared = pl.pallas_call(
        pack_kernel,
        out_shape=[
            jax.ShapeDtypeStruct((2 * tp_size, 4, chunk, lanes), BF16),
            jax.ShapeDtypeStruct((1,), jnp.int32),
        ],
        in_specs=[anywhere] * 5,
        out_specs=[anywhere] * 2,
        scratch_shapes=[
            pltpu.VMEM((4, chunk, width), BF16),
            pltpu.SMEM(tile_image.shape, jnp.int32),
            pltpu.SMEM((1,), jnp.int32),
            pltpu.SemaphoreType.DMA((4,)),
            pltpu.SemaphoreType.DMA,
            pltpu.SemaphoreType.DMA((2,)),
        ],
    )(tile_image, queries, keys, values, out_grad)
    groups = [
        [(left + place // tp_size) % seq_size * tp_size + place % tp_size for place in group_order(tp_size)]
        for left in range(1, seq_size, 2)
    ]

    def with_far(chunks):
        return lax.all_to_all(
            chunks, ("seq", "tp"), split_axis=0, concat_axis=0, tiled=True, axis_index_groups=groups
        )

    def own_only(chunks):
        mine = lax.all_to_all(chunks[::2], "tp", split_axis=0, concat_axis=0, tiled=True)
        return jnp.stack([mine, mine], axis=1).reshape(chunks.shape)

    pair = lax.cond(shared[0] > 0, with_far, own_only, doubled)
    is_right = 1 - seq_index % 2
    own = jnp.where(is_right == 1, pair[1::2], pair[::2])
    swaps = [(left, left + 1) for left in range(0, seq_size, 2)]
    near = lax.ppermute(own, "seq", swaps + [(right, left) for left, right in swaps])
    out = jax.ShapeDtypeStruct((row_count, lanes), BF16)
    heads = lanes // HEAD_DIM
    window = pltpu.VMEM((WINDOW * TILE // chunk, 4, chunk, lanes), BF16)
    squares = [pltpu.VMEM((WINDOW * TILE, WINDOW * TILE), BF16)] * (2 * heads)
    params = pltpu.CompilerParams(vmem_limit_bytes=24 * 1024 * 1024)
    work = heads * 2 * 12 * (WINDOW * TILE) ** 2 * HEAD_DIM
    cost = pl.CostEstimate(flops=work, bytes_accessed=pair.size * 2, transcendentals=heads * 2 * (WINDOW * TILE) ** 2)
    started = pl.pallas_call(
        far_kernel,
        out_shape=[out] * 4,
        in_specs=[smem, smem, vmem],
        out_specs=[vmem] * 4,
        scratch_shapes=[window, *squares],
        compiler_params=params,
        cost_estimate=cost,
    )(tile_image, pad_count, pair)
    return pl.pallas_call(
        near_kernel,
        out_shape=[out] * 4,
        in_specs=[smem, smem, vmem, vmem] + [anywhere] * 4,
        out_specs=[anywhere] * 4,
        scratch_shapes=[
            pltpu.VMEM((2, 4, TILE, lanes), BF16),
            window,
            pltpu.SemaphoreType.DMA((2, 4)),
            *squares,
        ],
        input_output_aliases={4 + index: index for index in range(4)},
        compiler_params=params,
    )(tile_image, pad_count, near, pair, *started)


def solution(mesh):
    rows = P(("seq", "tp"), None)
    out = P("seq", "tp")
    return jax.shard_map(
        body, mesh=mesh, in_specs=(rows,) * 4 + (P(), P()), out_specs=(out,) * 4, check_vma=False
    )
```
